256 devices in a mesh: tm: 32 (over y_lo, z, core), blk: 8 (over x, y_hi).
Axes of the slice: x: 4, y: 4 (y_hi: 2, y_lo: 2; y = y_hi * 2 + y_lo), z: 8, core: 2. Of those that a mesh axis runs over, the one named last changes fastest.
Arguments:
- psi_start: float32 [32, 8, 6, 8192], P('tm', 'blk'), may hold values from -6 to 6
- objective: float32 [32, 8, 6, 8192], P('tm', 'blk'), may hold values from -6 to 6
- jacobian: bfloat16 [32, 8, 6, 6, 6, 8192], P('tm', 'blk'), may hold values from -1 to 1
- precond: bfloat16 [32, 8, 6, 6, 8192], P('tm', 'blk'), may hold values from -0.8984375 to 0.8984375
- volume: float32 [8, 8192], P('blk'), may hold values from 0.02 to 0.2
- counts: int32 [8], P('blk'), may hold values from 4096 to 8192, as said below
- neighbours: int32 [8, 6, 8192], P('blk'), may hold values from 0 to 255
- donor: int32 [8, 512], P('blk'), may hold values from 0 to 4095
- match_block: int32 [32, 8, 4], P('tm', 'blk'), may hold values from 0 to 31
- slide: int32 [32, 8, 4], P('tm', 'blk'), may hold values from 0 to 127
Outputs:
- psi: float32 [32, 8, 6, 8192], P('tm', 'blk')
The draws below stay inside these ranges and needn't reach their ends.
Inputs may be any that keep to these rules, and one draw needn't show every extreme that they name: `counts`: every value lies in 4096 to 8192; some partition holds exactly 8192 live cells.
All inputs are finite; a program needn't handle non-finite values.
Results may differ from the reference program's by a relative error of at most 0.0004.
Values sent between devices are 32-bit elements; how exact they have to be, the bound alone decides.
No kernel may reach another device: no remote copies, remote signals or barrier semaphores. Data moves between devices by JAX's collectives and lax.ppermute only.
A program may use at most 64 MiB of HBM per device.

```python
import math
import jax
import jax.numpy as jnp
from jax import lax

F = 6
K = 6
SWEEPS = 2
CELLS = 8192
IFB = 4
IFACES = 512
NT = 32
NB = 8
N_TM = 32
N_BLK = 8


def draw_counts(key, part):
    key = jax.random.fold_in(key, 1)
    values = jax.random.randint(key, (NB,), CELLS // 2, CELLS + 1)
    fullest = jax.random.randint(jax.random.fold_in(key, 2), (), 0, NB)
    return jnp.where(jnp.arange(NB) == fullest, CELLS, values).astype(jnp.int32)


def with_ends(entries, key, least, top_value):
    longest = entries.shape.index(max(entries.shape))
    spots = []
    for shift in (0, 1):
        where = [jax.random.randint(jax.random.fold_in(key, axis), (), 0, length) for axis, length in enumerate(entries.shape)]
        where[longest] = (where[longest] + shift) % entries.shape[longest]
        spots.append(tuple(where))
    return entries.at[spots[0]].set(least).at[spots[1]].set(top_value)


def shard_levels(key, extent, cuts, least, largest):
    def one(axis_at, shards_of):
        draws = jax.random.uniform(jax.random.fold_in(jax.random.fold_in(key, 6), axis_at), (shards_of,), jnp.float32, least / len(cuts), largest / len(cuts))
        return jnp.repeat(jnp.exp(draws), extent[axis_at] // shards_of).reshape((-1,) + (1,) * (len(extent) - axis_at - 1))

    gain = one(*cuts[0])
    for cut in cuts[1:]:
        gain = gain * one(*cut)
    return gain


def scatter_about(rng, shape, width, bound, shards=(), kind=jnp.bfloat16):
    level = shard_levels(rng, shape, shards, -0.22, 0.18) if shards else 1.0
    values = jax.random.normal(rng, shape, jnp.float32) * width * level
    return jnp.minimum(jnp.maximum(values, -bound), bound).astype(kind)


def setup_inputs(seed: int = 0) -> dict:
    key_of = jax.random.split(jax.random.key(seed), 11)
    return {
        "psi_start": scatter_about(key_of[0], (NT, NB, F, CELLS), 1.0, 6.0, ((0, 32), (1, 8)), jnp.float32),
        "objective": scatter_about(key_of[1], (NT, NB, F, CELLS), 1.0, 6.0, ((0, 32), (1, 8)), jnp.float32),
        "jacobian": scatter_about(key_of[2], (NT, NB, F, F, K, CELLS), (F * K) ** -0.5, 1.0, ((0, 32), (1, 8))),
        "precond": scatter_about(key_of[3], (NT, NB, F, F, CELLS), 0.15, 0.8984375, ((0, 32), (1, 8))),
        "volume": jnp.clip(jnp.exp(math.log(0.2) - 2.3025851 * jax.random.uniform(key_of[4], (NB, CELLS), jnp.float32) ** shard_levels(key_of[4], (NB, CELLS), ((0, 8),), -0.2, 0.2)), 0.02, 0.2),
        "counts": draw_counts(jax.random.fold_in(key_of[10], 71), 0),
        "neighbours": with_ends(jax.random.randint(key_of[6], (NB, K, CELLS), 0, 256), jax.random.fold_in(key_of[6], 1), 0, 255).astype(jnp.int32),
        "donor": with_ends(jax.random.randint(key_of[7], (NB, IFACES), 0, CELLS // 2), jax.random.fold_in(key_of[7], 1), 0, (CELLS // 2) - 1).astype(jnp.int32),
        "match_block": with_ends(jax.random.randint(key_of[8], (NT, NB, IFB), 0, NB * IFB), jax.random.fold_in(key_of[8], 1), 0, (NB * IFB) - 1).astype(jnp.int32),
        "slide": with_ends(jax.random.randint(key_of[9], (NT, NB, IFB), 0, 128), jax.random.fold_in(key_of[9], 1), 0, 127).astype(jnp.int32),
    }


def time_matrix(count):
    index = jnp.arange(count)
    offset = index[:, None] - index[None, :]
    angle = math.pi * offset.astype(jnp.float32) / count
    parity = jnp.where(offset % 2 == 0, 1.0, -1.0).astype(jnp.float32)
    safe_angle = jnp.where(offset == 0, 0.5 * math.pi, angle)
    sine = jnp.sin(safe_angle)
    value = 0.5 * parity * jnp.cos(safe_angle) / sine + 0.125 * parity / (sine * sine)
    diagonal_value = 0.25 * (count * count + 2) / 12.0
    return jnp.where(offset == 0, diagonal_value, value).astype(jnp.float32)


def face_source(match_block, slide):
    within = jnp.arange(128)
    full = match_block[..., None] * 128 + (within + slide[..., None]) % 128
    return full.reshape(match_block.shape[:-1] + (match_block.shape[-1] * 128,)).astype(jnp.int32)


def reference(psi_start, objective, jacobian, precond, volume, counts, neighbours, donor, match_block, slide):
    live = (jnp.arange(CELLS)[None, :] < counts[:, None]).astype(jnp.float32)
    psi = psi_start * live[None, :, None, :]
    d = time_matrix(N_TM)
    source = face_source(match_block, slide)
    cell_block = (jnp.arange(CELLS) // 128).astype(jnp.int32)
    place = jnp.where(neighbours < 128, cell_block * 128 + neighbours,
                      CELLS + (cell_block % IFB) * 128 + neighbours - 128).astype(jnp.int32)
    for sweep in range(SWEEPS):
        index = jnp.broadcast_to(donor[None, :, None, :], (N_TM, N_BLK, F, IFACES))
        donors = jnp.take_along_axis(psi, index, axis=3)
        pool = donors.transpose(0, 2, 1, 3).reshape(N_TM, F, N_BLK * IFACES)
        ghost_index = jnp.broadcast_to(source[:, :, None, :], (N_TM, N_BLK, F, IFACES))
        ghost = jnp.take_along_axis(jnp.broadcast_to(pool[:, None], (N_TM, N_BLK, F, N_BLK * IFACES)), ghost_index, axis=3)
        extended = jnp.concatenate([psi, ghost], axis=3)
        coupling = jnp.einsum('st,sbfc->tbfc', d, psi, precision=lax.Precision.HIGHEST)

        def slice_flux(items):
            ext_slice, jac_slice, pre_slice, cpl_slice, obj_slice, psi_slice = items
            values = jax.vmap(lambda ext_part, nbr_part: ext_part[:, nbr_part])(ext_slice, place)
            flux = jnp.sum(jac_slice.astype(jnp.float32) * values[:, None], axis=(2, 3))
            residual = flux + volume[:, None, :] * cpl_slice - obj_slice
            update = jnp.sum(pre_slice.astype(jnp.float32) * residual[:, None], axis=2)
            return (psi_slice - update) * live[:, None, :]

        psi = lax.map(slice_flux, (extended, jacobian, precond, coupling, objective, psi))
    return psi
```

```python
import math

import numpy as np
import jax
import jax.numpy as jnp
from jax import lax
from jax.experimental import pallas as pl
from jax.experimental.pallas import tpu as pltpu
from jax.sharding import PartitionSpec as P

SWEEPS = 2
F = 6
K = 6
CELLS = 8192
GROUPS = 64
ROWS = F * GROUPS
NT = 32
CHIPS = 16
CHUNK = ROWS // CHIPS
VMEM = pl.BlockSpec(memory_space=pltpu.VMEM)
SMEM = pl.BlockSpec(memory_space=pltpu.SMEM)
ANY = pl.BlockSpec(memory_space=pl.ANY)


def time_kernel():
    n = np.arange(NT)
    parity = np.where(n % 2 == 0, 1.0, -1.0)
    angle = np.where(n == 0, 0.5 * math.pi, math.pi * n / NT)
    sine = np.sin(angle)
    value = 0.5 * parity * np.cos(angle) / sine + 0.125 * parity / (sine * sine)
    return np.where(n == 0, 0.25 * (NT * NT + 2) / 12.0, value).astype(np.float32)


def params(mib=12):
    return pltpu.CompilerParams(vmem_limit_bytes=mib * 1024 * 1024)


def cost(flops, nbytes):
    return pl.CostEstimate(flops=flops, bytes_accessed=nbytes, transcendentals=0)


def f32_rows(n):
    return jax.ShapeDtypeStruct((n, 128), jnp.float32)


def i32_rows(n):
    return jax.ShapeDtypeStruct((n, 128), jnp.int32)


def lane_gather(data, index):
    return jnp.take_along_axis(data, index, axis=1, mode="promise_in_bounds")


def tile(start):
    return pl.ds(pl.multiple_of(start, 8), 8)


def fetch_donor_kernel(psi_hbm, donor_hbm, sent_ref, psi_ref, donor_ref, sems):
    copies = [pltpu.make_async_copy(donor_hbm, donor_ref, sems.at[0]), pltpu.make_async_copy(psi_hbm, psi_ref, sems.at[1])]
    for copy in copies:
        copy.start()
    for copy in copies:
        copy.wait()
    donor_kernel(psi_ref, donor_ref, sent_ref)


def donor_kernel(psi_ref, donor_ref, sent_ref):
    sublane = lax.broadcasted_iota(jnp.int32, (8, 128), 0)

    def block(q, carry):
        donor = jnp.broadcast_to(donor_ref[pl.ds(q, 1), :], (8, 128))
        lane = donor & 127
        home = (donor >> 7) - sublane
        rows = []
        for f in range(F):
            total = jnp.zeros((8, 128), jnp.float32)
            for b in range(4):
                picked = lane_gather(psi_ref[pl.ds(f * GROUPS + b * 8, 8), :], lane)
                total = total + jnp.where(home == b * 8, picked, 0.0)
            rows.append(jnp.sum(total, axis=0, keepdims=True))
        rows.append(jnp.zeros((2, 128), jnp.float32))
        sent_ref[tile(q * 8), :] = jnp.concatenate(rows, axis=0)
        return carry

    lax.fori_loop(0, 4, block, 0, unroll=2)


def pack_donors(fetch, psi, donor):
    scratch = [pltpu.VMEM((ROWS, 128), jnp.float32), pltpu.VMEM((4, 128), jnp.int32), pltpu.SemaphoreType.DMA((2,))]
    return pl.pallas_call(
        fetch_donor_kernel if fetch else donor_kernel,
        out_shape=f32_rows(32),
        in_specs=[ANY, ANY] if fetch else [VMEM, VMEM],
        out_specs=VMEM,
        scratch_shapes=scratch if fetch else [],
        compiler_params=params(58 if fetch else 12),
        cost_estimate=cost(400000, 220000),
        name="pack_donors",
    )(psi, donor)


def merge_kernel(*refs):
    for n in range(4):
        refs[4][pl.ds(n * 32, 32), :] = refs[n][...]


def merge(*pieces):
    return pl.pallas_call(
        merge_kernel,
        out_shape=f32_rows(128),
        in_specs=[VMEM] * 4,
        out_specs=VMEM,
        compiler_params=params(),
        cost_estimate=cost(30000000000, 130000),
        name="merge",
    )(*pieces)


def prepare_kernel(
    counts_hbm, match_hbm, slide_hbm, pre_hbm, nbr_hbm, volume_hbm,
    dense_ref, stencil_ref, live_ref, scale_ref, route_ref,
    pre_ref, nbr_ref, volume_ref, counts_ref, match_ref, slide_ref, sems
):
    scalars = [
        pltpu.make_async_copy(counts_hbm, counts_ref, sems.at[3]),
        pltpu.make_async_copy(match_hbm, match_ref, sems.at[4]),
        pltpu.make_async_copy(slide_hbm, slide_ref, sems.at[5]),
    ]
    copies = [
        pltpu.make_async_copy(nbr_hbm, nbr_ref, sems.at[0]),
        pltpu.make_async_copy(volume_hbm, volume_ref, sems.at[1]),
        pltpu.make_async_copy(pre_hbm, pre_ref, sems.at[2]),
    ]
    for copy in scalars + copies:
        copy.start()
    for copy in scalars:
        copy.wait()
    own = lax.axis_index("blk")
    sublane = lax.broadcasted_iota(jnp.int32, (8, 128), 0)
    lane = lax.broadcasted_iota(jnp.int32, (8, 128), 1)
    place = jnp.zeros((8, 128), jnp.int32)
    turn = jnp.zeros((8, 128), jnp.int32)
    for q in range(4):
        block = match_ref[q]
        part = block // 4
        hop = (part // 2) ^ (own // 2)
        side = lax.rem(part, 2) ^ lax.rem(own, 2)
        place = jnp.where(sublane == q, side * 16 + hop * 4 + lax.rem(block, 4), place)
        turn = jnp.where(sublane == q, slide_ref[q], turn)
    route_ref[pl.ds(0, 8), :] = place
    route_ref[pl.ds(8, 8), :] = (lane + turn) & 127
    stencil_ref[...] = jnp.zeros_like(stencil_ref)
    copies[0].wait()
    for k in range(K):
        for b in range(8):
            stencil_ref[pl.ds(b * 64 + k, 8, stride=8), :] = nbr_ref[pl.ds(k * GROUPS + b * 8, 8), :]
    copies[1].wait()
    for b in range(8):
        live = jnp.where(sublane * 128 + lane + b * 1024 < counts_ref[0], 1.0, 0.0)
        live_ref[pl.ds(b * 8, 8), :] = live
        scale_ref[pl.ds(b * 8, 8), :] = live * volume_ref[pl.ds(b * 8, 8), :]
    copies[2].wait()

    def step(g, carry):
        at = pl.multiple_of(g * 128, 128)
        for i in range(F):
            dense_ref[pl.ds(i * F * GROUPS + g, F, stride=GROUPS), :] = pre_ref[i, :, pl.ds(at, 128)].astype(jnp.float32)
        return carry

    lax.fori_loop(0, GROUPS, step, 0, unroll=4)


def prepare(counts, match, slide, precond, neighbours, volume):
    return pl.pallas_call(
        prepare_kernel,
        out_shape=(f32_rows(F * F * GROUPS), i32_rows(GROUPS * 8), f32_rows(GROUPS), f32_rows(GROUPS), i32_rows(16)),
        in_specs=[ANY] * 6,
        out_specs=(VMEM,) * 5,
        scratch_shapes=[
            pltpu.VMEM((F, F, CELLS), jnp.bfloat16),
            pltpu.VMEM((ROWS, 128), jnp.int32),
            pltpu.VMEM((GROUPS, 128), jnp.float32),
            pltpu.SMEM((1,), jnp.int32),
            pltpu.SMEM((4,), jnp.int32),
            pltpu.SMEM((4,), jnp.int32),
            pltpu.SemaphoreType.DMA((6,)),
        ],
        compiler_params=params(58),
        cost_estimate=cost(1000000, 2500000),
        name="prepare",
    )(counts, match, slide, precond, neighbours, volume)


def flux_kernel(
    psi_hbm, target_hbm, jac_hbm, near_ref, far_ref, route_ref, live_ref, stencil_ref, dense_ref,
    out_ref, psi_s, target_s, jac_s, ghost_s, part_s, sems
):
    first = pltpu.make_async_copy(psi_hbm, psi_s, sems.at[8])
    first.start()

    def jac_copy(b):
        cells = pl.ds(pl.multiple_of(b * 1024, 1024), 1024)
        return pltpu.make_async_copy(jac_hbm.at[:, :, :, cells], jac_s.at[:, :, :, cells], sems.at[b])

    for b in range(8):
        jac_copy(b).start()
    last = pltpu.make_async_copy(target_hbm, target_s, sems.at[9])
    last.start()
    for q in range(4):
        place = jnp.broadcast_to(route_ref[pl.ds(q, 1), :], (8, 128))
        source = jnp.zeros((8, 128), jnp.float32)
        for n in range(16):
            source = jnp.where(place == n, near_ref[pl.ds(n * 8, 8), :], source)
            source = jnp.where(place == 16 + n, far_ref[pl.ds(n * 8, 8), :], source)
        turn = jnp.broadcast_to(route_ref[pl.ds(8 + q, 1), :], (8, 128))
        ghost_s[pl.ds(q * 8, 8), :] = lane_gather(source, turn)
    first.wait()
    for b in range(8):
        live = live_ref[pl.ds(b * 8, 8), :]
        for f in range(F):
            rows = pl.ds(f * GROUPS + b * 8, 8)
            psi_s[rows, :] = psi_s[rows, :] * live

    def step(b, carry):
        jac_copy(b).wait()
        for s in range(8):
            g = b * 8 + s
            at = pl.multiple_of(g * 128, 128)
            index = stencil_ref[tile(g * 8), :]
            outside = index >= 128
            pick = index & 127
            total = [None] * F
            for j in range(F):
                inner = jnp.broadcast_to(psi_s[pl.ds(j * GROUPS + g, 1), :], (8, 128))
                outer = jnp.broadcast_to(ghost_s[pl.ds((s % 4) * 8 + j, 1), :], (8, 128))
                value = jnp.where(outside, lane_gather(outer, pick), lane_gather(inner, pick))[:K]
                for i in range(F):
                    term = jac_s[i, j, :, pl.ds(at, 128)].astype(jnp.float32) * value
                    total[i] = term if j == 0 else total[i] + term
            for i in range(F):
                part_s[pl.ds(pl.multiple_of(g * 48 + i * 8, 8), K), :] = total[i]
        return carry

    lax.fori_loop(0, 8, step, 0)
    last.wait()

    def finish(b, carry):
        live = live_ref[tile(b * 8), :]
        residual = []
        for j in range(F):
            flux = part_s[pl.ds(b * 384 + j * 8, 8, stride=48), :]
            for k in range(1, K):
                flux = flux + part_s[pl.ds(b * 384 + j * 8 + k, 8, stride=48), :]
            residual.append(flux - target_s[tile(j * GROUPS + b * 8), :])
        for i in range(F):
            rows = tile(i * GROUPS + b * 8)
            value = psi_s[rows, :]
            for j in range(F):
                value = value - dense_ref[tile((i * F + j) * GROUPS + b * 8), :] * residual[j]
            out_ref[rows, :] = live * value
        return carry

    lax.fori_loop(0, 8, finish, 0)


def flux_part(psi, target, jac, near, far, route, live, stencil, dense):
    return pl.pallas_call(
        flux_kernel,
        out_shape=f32_rows(ROWS),
        in_specs=[ANY] * 3 + [VMEM] * 6,
        out_specs=VMEM,
        scratch_shapes=[
            pltpu.VMEM((ROWS, 128), jnp.float32),
            pltpu.VMEM((ROWS, 128), jnp.float32),
            pltpu.VMEM((F, F, K, CELLS), jnp.bfloat16),
            pltpu.VMEM((32, 128), jnp.float32),
            pltpu.VMEM((GROUPS * 48, 128), jnp.float32),
            pltpu.SemaphoreType.DMA((10,)),
        ],
        compiler_params=params(50),
        cost_estimate=cost(30000000000, 7000000),
        name="flux_part",
    )(psi, target, jac, near, far, route, live, stencil, dense)


def couple_kernel(own_ref, other_ref, out_ref):
    f = [float(v) for v in time_kernel()]
    first = lax.rem(lax.axis_index("tm"), 2) == 0
    even = f[0::2]
    odd = [jnp.where(first, f[2 * n + 1], f[2 * n - 1]) for n in range(CHIPS)]
    for t0 in range(0, CHIPS, 8):
        for r in range(CHUNK // 8):
            total = [None] * 8
            for s in range(CHIPS):
                own = own_ref[pl.ds(s * CHUNK + r * 8, 8), :]
                other = other_ref[pl.ds(s * CHUNK + r * 8, 8), :]
                for t in range(8):
                    n = (s - t0 - t) % CHIPS
                    term = even[n] * own + odd[n] * other
                    total[t] = term if s == 0 else total[t] + term
            for t in range(8):
                out_ref[pl.ds((t0 + t) * CHUNK + r * 8, 8), :] = total[t]


def couple(own, other):
    return pl.pallas_call(
        couple_kernel,
        out_shape=f32_rows(ROWS),
        in_specs=[VMEM, VMEM],
        out_specs=VMEM,
        compiler_params=params(),
        cost_estimate=cost(3200000, 600000),
        name="couple",
    )(own, other)


def finish_kernel(base_ref, coupling_ref, scale_ref, dense_ref, out_ref):
    def step(b, carry):
        scale = scale_ref[tile(b * 8), :]
        term = [scale * coupling_ref[tile(j * GROUPS + b * 8), :] for j in range(F)]
        for i in range(F):
            rows = tile(i * GROUPS + b * 8)
            value = base_ref[rows, :]
            for j in range(F):
                value = value - dense_ref[tile((i * F + j) * GROUPS + b * 8), :] * term[j]
            out_ref[rows, :] = value
        return carry

    lax.fori_loop(0, 8, step, 0)


def finish(base, coupling, scale, dense):
    return pl.pallas_call(
        finish_kernel,
        out_shape=f32_rows(ROWS),
        in_specs=[VMEM] * 4,
        out_specs=VMEM,
        compiler_params=params(),
        cost_estimate=cost(600000, 2000000),
        name="finish",
    )(base, coupling, scale, dense)


def local(
    psi_start, objective, jacobian, precond, volume, counts, neighbours, donor, match_block, slide
):
    by_core = [[2 * chip + core for chip in range(CHIPS)] for core in range(2)]
    swap_core = [(i, i ^ 1) for i in range(NT)]

    def across(x):
        moved = lax.all_to_all(x.reshape(CHIPS, CHUNK, 128), "tm", 0, 0, axis_index_groups=by_core)
        return moved.reshape(ROWS, 128)
    def blk_swap(x, bits):
        return lax.ppermute(x, "blk", [(i, i ^ bits) for i in range(8)])

    psi = psi_start.reshape(ROWS, 128)
    target = objective.reshape(ROWS, 128)
    faces = donor.reshape(4, 128)
    dense, stencil, live, scale, route = prepare(
        counts, match_block.reshape(4), slide.reshape(4),
        precond[0, 0], neighbours.reshape(ROWS, 128), volume.reshape(GROUPS, 128)
    )
    for sweep in range(SWEEPS):
        states = across(psi)
        sent = pack_donors(sweep == 0, psi, faces)
        near = merge(sent, *[blk_swap(sent, 2 * hop) for hop in (1, 2, 3)])
        states, near, dense = lax.optimization_barrier((states, near, dense))
        coupling = across(couple(states, lax.ppermute(states, "tm", swap_core)))
        far = blk_swap(near, 1)
        base = flux_part(psi, target, jacobian[0, 0], near, far, route, live, stencil, dense)
        psi = finish(base, coupling, scale, dense)
    return psi.reshape(1, 1, F, CELLS)


def solution(mesh):
    in_specs = (
        P("tm", "blk", None, None),
        P("tm", "blk", None, None),
        P("tm", "blk", None, None, None, None),
        P("tm", "blk", None, None, None),
        P("blk", None),
        P("blk"),
        P("blk", None, None),
        P("blk", None),
        P("tm", "blk", None),
        P("tm", "blk", None),
    )
    out_specs = P("tm", "blk", None, None)
    return jax.shard_map(local, mesh=mesh, in_specs=in_specs, out_specs=out_specs, check_vma=False)
```

```python
import math

import numpy as np
import jax
import jax.numpy as jnp
from jax import lax
from jax.experimental import pallas as pl
from jax.experimental.pallas import tpu as pltpu
from jax.sharding import PartitionSpec as P

SWEEPS = 2
FLUXHINTS = (30000000000, 6000000)
MERGEHINTS = (30000000000, 65536)
LATE = 1
BIGHINT = 30000000000
F = 6
K = 6
CELLS = 8192
GROUPS = 64
STRIDE = 72
UNROLL = 16
HOPS = (0, 1, 3, 2)
ROWS = F * GROUPS
NT = 32
CHIPS = 16
CHUNK = ROWS // CHIPS
VMEM = pl.BlockSpec(memory_space=pltpu.VMEM)
SMEM = pl.BlockSpec(memory_space=pltpu.SMEM)
ANY = pl.BlockSpec(memory_space=pl.ANY)


def time_kernel():
    n = np.arange(NT)
    parity = np.where(n % 2 == 0, 1.0, -1.0)
    angle = np.where(n == 0, 0.5 * math.pi, math.pi * n / NT)
    sine = np.sin(angle)
    value = 0.5 * parity * np.cos(angle) / sine + 0.125 * parity / (sine * sine)
    return np.where(n == 0, 0.25 * (NT * NT + 2) / 12.0, value).astype(np.float32)


def params(mib=12):
    return pltpu.CompilerParams(vmem_limit_bytes=mib * 1024 * 1024)


def cost(flops, nbytes):
    return pl.CostEstimate(flops=flops, bytes_accessed=nbytes, transcendentals=0)


def f32_rows(n):
    return jax.ShapeDtypeStruct((n, 128), jnp.float32)


def i32_rows(n):
    return jax.ShapeDtypeStruct((n, 128), jnp.int32)


def lane_gather(data, index):
    return jnp.take_along_axis(data, index, axis=1, mode="promise_in_bounds")


def tile(start):
    return pl.ds(pl.multiple_of(start, 8), 8)


def fetch_donor_kernel(psi_hbm, donor_hbm, sent_ref, psi_ref, donor_ref, sems):
    copies = [pltpu.make_async_copy(donor_hbm, donor_ref, sems.at[F])]
    for f in range(F):
        rows = pl.ds(f * GROUPS, GROUPS // 2)
        copies.append(pltpu.make_async_copy(psi_hbm.at[rows, :], psi_ref.at[rows, :], sems.at[f]))
    for copy in copies:
        copy.start()
    for copy in copies:
        copy.wait()
    donor_kernel(psi_ref, donor_ref, sent_ref)


def donor_kernel(psi_ref, donor_ref, sent_ref):
    sublane = lax.broadcasted_iota(jnp.int32, (8, 128), 0)

    def block(q, carry):
        donor = jnp.broadcast_to(donor_ref[pl.ds(q, 1), :], (8, 128))
        lane = donor & 127
        home = (donor >> 7) - sublane
        rows = []
        for f in range(F):
            total = jnp.zeros((8, 128), jnp.float32)
            for b in range(4):
                picked = lane_gather(psi_ref[pl.ds(f * GROUPS + b * 8, 8), :], lane)
                total = total + jnp.where(home == b * 8, picked, 0.0)
            rows.append(jnp.sum(total, axis=0, keepdims=True))
        rows.append(jnp.zeros((2, 128), jnp.float32))
        sent_ref[tile(q * 8), :] = jnp.concatenate(rows, axis=0)
        return carry

    lax.fori_loop(0, 4, block, 0, unroll=2)


def pack_donors(psi, donor):
    return pl.pallas_call(
        fetch_donor_kernel,
        out_shape=f32_rows(32),
        in_specs=[ANY, ANY],
        out_specs=VMEM,
        scratch_shapes=[
            pltpu.VMEM((ROWS, 128), jnp.float32),
            pltpu.VMEM((4, 128), jnp.int32),
            pltpu.SemaphoreType.DMA((F + 1,)),
        ],
        compiler_params=params(58),
        cost_estimate=cost(400000, 220000),
        name="pack_donors",
    )(psi, donor)


def merge_kernel(*refs):
    height = refs[0].shape[0]
    for n in range(refs[-1].shape[0] // height):
        refs[-1][pl.ds(n * height, height), :] = refs[n][...]


def merge(hint, pieces, ready=()):
    return pl.pallas_call(
        merge_kernel,
        out_shape=f32_rows(sum(piece.shape[0] for piece in pieces)),
        in_specs=[VMEM] * len(pieces) + [ANY] * len(ready),
        out_specs=VMEM,
        compiler_params=params(),
        cost_estimate=cost(hint, 65536),
        name="merge",
    )(*pieces, *ready)


def prepare_kernel(counts_hbm, pre_hbm, volume_hbm, after_ref, dense_ref, live_ref, scale_ref, pre_ref, volume_ref, counts_ref, sems):
    copies = [
        pltpu.make_async_copy(counts_hbm, counts_ref, sems.at[0]),
        pltpu.make_async_copy(volume_hbm, volume_ref, sems.at[1]),
        pltpu.make_async_copy(pre_hbm, pre_ref, sems.at[2]),
    ]
    for copy in copies:
        copy.start()
    copies[0].wait()
    copies[1].wait()
    for b in range(8):
        live = live_rows(counts_ref, b)
        live_ref[pl.ds(b * 8, 8), :] = live
        scale_ref[pl.ds(b * 8, 8), :] = live * volume_ref[pl.ds(b * 8, 8), :]
    copies[2].wait()

    def step(g, carry):
        at = pl.multiple_of(g * 128, 128)
        for i in range(F):
            dense_ref[pl.ds(i * F * STRIDE + g, F, stride=STRIDE), :] = pre_ref[i, :, pl.ds(at, 128)].astype(jnp.float32)
        return carry

    lax.fori_loop(0, GROUPS, step, 0, unroll=8)


def prepare(counts, precond, volume, after):
    return pl.pallas_call(
        prepare_kernel,
        out_shape=(f32_rows(F * F * STRIDE), f32_rows(GROUPS), f32_rows(GROUPS)),
        in_specs=[ANY] * 4,
        out_specs=(VMEM,) * 3,
        scratch_shapes=[
            pltpu.VMEM((F, F, CELLS), jnp.bfloat16),
            pltpu.VMEM((GROUPS, 128), jnp.float32),
            pltpu.SMEM((1,), jnp.int32),
            pltpu.SemaphoreType.DMA((3,)),
        ],
        compiler_params=params(50),
        cost_estimate=cost(1000000, 2500000),
        name="prepare",
    )(counts, precond, volume, after)


def live_rows(counts_ref, block):
    cell = lax.broadcasted_iota(jnp.int32, (8, 128), 0) * 128 + lax.broadcasted_iota(jnp.int32, (8, 128), 1)
    return jnp.where(cell + block * 1024 < counts_ref[0], 1.0, 0.0)


def flux_kernel(
    counts_hbm, match_hbm, slide_hbm, psi_hbm, nbr_hbm, target_hbm, jac_hbm, *refs
):
    pieces = refs[:-13]
    (out_ref, psi_s, counts_ref, match_ref, slide_ref, nbr_s, target_s, jac_s, stencil_s, pool_s, ghost_s, part_s, sems) = refs[-13:]
    small = [
        pltpu.make_async_copy(counts_hbm, counts_ref, sems.at[8]),
        pltpu.make_async_copy(match_hbm, match_ref, sems.at[9]),
        pltpu.make_async_copy(slide_hbm, slide_ref, sems.at[10]),
    ]
    nbr_copy = pltpu.make_async_copy(nbr_hbm, nbr_s, sems.at[11])
    psi_copy = pltpu.make_async_copy(psi_hbm, psi_s, sems.at[12])
    target_copy = pltpu.make_async_copy(target_hbm, target_s, sems.at[13])

    def jac_copy(b):
        cells = pl.ds(pl.multiple_of(b * 1024, 1024), 1024)
        return pltpu.make_async_copy(jac_hbm.at[:, :, :, cells], jac_s.at[:, :, :, cells], sems.at[b])

    for copy in small:
        copy.start()
    nbr_copy.start()
    psi_copy.start()
    for b in range(8):
        jac_copy(b).start()
    target_copy.start()
    hops = iter(HOPS)
    for piece in pieces:
        for n in range(piece.shape[0] // 64):
            pool_s[pl.ds(next(hops) * 64, 64), :] = piece[pl.ds(n * 64, 64), :]
    stencil_s[...] = jnp.zeros_like(stencil_s)
    own = lax.axis_index("blk")
    lane = lax.broadcasted_iota(jnp.int32, (8, 128), 1)
    for copy in small:
        copy.wait()
    for q in range(4):
        block = match_ref[q]
        part = block // 4
        hop = (part // 2) ^ (own // 2)
        side = lax.rem(part, 2) ^ lax.rem(own, 2)
        source = pool_s[tile((hop * 8 + side * 4 + lax.rem(block, 4)) * 8), :]
        ghost_s[pl.ds(q * 8, 8), :] = lane_gather(source, (lane + slide_ref[q]) & 127)
    nbr_copy.wait()
    for k in range(K):
        for b in range(8):
            stencil_s[pl.ds(b * 64 + k, 8, stride=8), :] = nbr_s[pl.ds(k * GROUPS + b * 8, 8), :]
    psi_copy.wait()
    for b in range(8):
        live = live_rows(counts_ref, b)
        for f in range(F):
            rows = pl.ds(f * GROUPS + b * 8, 8)
            psi_s[rows, :] = psi_s[rows, :] * live

    def step(b, carry):
        for n in range(UNROLL // 8):
            jac_copy(b * (UNROLL // 8) + n).wait()
        for s in range(UNROLL):
            g = b * UNROLL + s
            at = pl.multiple_of(g * 128, 128)
            index = stencil_s[tile(g * 8), :]
            outside = index >= 128
            pick = index & 127
            total = [None] * F
            for j in range(F):
                inner = jnp.broadcast_to(psi_s[pl.ds(j * GROUPS + g, 1), :], (8, 128))
                outer = jnp.broadcast_to(ghost_s[pl.ds((s % 4) * 8 + j, 1), :], (8, 128))
                value = jnp.where(outside, lane_gather(outer, pick), lane_gather(inner, pick))[:K]
                for i in range(F):
                    term = jac_s[i, j, :, pl.ds(at, 128)].astype(jnp.float32) * value
                    total[i] = term if j == 0 else total[i] + term
            for i in range(F):
                part_s[pl.ds(pl.multiple_of(g * 48 + i * 8, 8), K), :] = total[i]
        return carry

    lax.fori_loop(0, GROUPS // UNROLL, step, 0)
    target_copy.wait()

    def gather_up(b, carry):
        for j in range(F):
            flux = part_s[pl.ds(b * 384 + j * 8, 8, stride=48), :]
            for k in range(1, K):
                flux = flux + part_s[pl.ds(b * 384 + j * 8 + k, 8, stride=48), :]
            rows = tile(j * GROUPS + b * 8)
            out_ref[rows, :] = flux - target_s[rows, :]
        return carry

    lax.fori_loop(0, 8, gather_up, 0, unroll=2)


def flux_part(hint, counts, match, slide, psi, neighbours, target, jac, pieces):
    return pl.pallas_call(
        flux_kernel,
        out_shape=(f32_rows(ROWS), f32_rows(ROWS)),
        in_specs=[ANY] * 7 + [VMEM] * len(pieces),
        out_specs=(VMEM, VMEM),
        scratch_shapes=[
            pltpu.SMEM((1,), jnp.int32),
            pltpu.SMEM((4,), jnp.int32),
            pltpu.SMEM((4,), jnp.int32),
            pltpu.VMEM((ROWS, 128), jnp.int32),
            pltpu.VMEM((ROWS, 128), jnp.float32),
            pltpu.VMEM((F, F, K, CELLS), jnp.bfloat16),
            pltpu.VMEM((GROUPS * 8, 128), jnp.int32),
            pltpu.VMEM((256, 128), jnp.float32),
            pltpu.VMEM((32, 128), jnp.float32),
            pltpu.VMEM((GROUPS * 48, 128), jnp.float32),
            pltpu.SemaphoreType.DMA((14,)),
        ],
        compiler_params=params(50),
        cost_estimate=cost(hint, 7000000),
        name="flux_part",
    )(counts, match, slide, psi, neighbours, target, jac, *pieces)


def couple_kernel(own_ref, other_ref, out_ref):
    f = [float(v) for v in time_kernel()]
    first = lax.rem(lax.axis_index("tm"), 2) == 0
    even = f[0::2]
    odd = [jnp.where(first, f[2 * n + 1], f[2 * n - 1]) for n in range(CHIPS)]
    for t0 in range(0, CHIPS, 8):
        for r in range(CHUNK // 8):
            total = [None] * 8
            for s in range(CHIPS):
                own = own_ref[pl.ds(s * CHUNK + r * 8, 8), :]
                other = other_ref[pl.ds(s * CHUNK + r * 8, 8), :]
                for t in range(8):
                    n = (s - t0 - t) % CHIPS
                    term = even[n] * own + odd[n] * other
                    total[t] = term if s == 0 else total[t] + term
            for t in range(8):
                out_ref[pl.ds((t0 + t) * CHUNK + r * 8, 8), :] = total[t]


def couple(own, other):
    return pl.pallas_call(
        couple_kernel,
        out_shape=f32_rows(ROWS),
        in_specs=[VMEM, VMEM],
        out_specs=VMEM,
        compiler_params=params(),
        cost_estimate=cost(3200000, 600000),
        name="couple",
    )(own, other)


def finish_kernel(base_ref, residual_ref, coupling_ref, live_ref, scale_ref, dense_ref, *rest):
    out_ref = rest[-1] if len(rest) == 1 else rest[1]

    def step(b, carry):
        live = live_ref[tile(b * 8), :]
        scale = scale_ref[tile(b * 8), :]
        whole = []
        for j in range(F):
            rows = tile(j * GROUPS + b * 8)
            whole.append(live * residual_ref[rows, :] + scale * coupling_ref[rows, :])
        for i in range(F):
            rows = tile(i * GROUPS + b * 8)
            value = base_ref[rows, :]
            for j in range(F):
                value = value - dense_ref[tile((i * F + j) * STRIDE + b * 8), :] * whole[j]
            out_ref[rows, :] = value
        return carry

    lax.fori_loop(0, 8, step, 0)
    if len(rest) > 1:
        donor_kernel(out_ref, rest[0], rest[2])


def finish(base, residual, coupling, live, scale, dense, donor=None):
    operands = [base, residual, coupling, live, scale, dense] + ([] if donor is None else [donor])
    shapes = [f32_rows(ROWS)] + ([] if donor is None else [f32_rows(32)])
    return pl.pallas_call(
        finish_kernel,
        out_shape=shapes,
        in_specs=[VMEM] * len(operands),
        out_specs=[VMEM] * len(shapes),
        compiler_params=params(),
        cost_estimate=cost(600000, 2000000),
        name="finish",
    )(*operands)


def local(
    psi_start, objective, jacobian, precond, volume, counts, neighbours, donor, match_block, slide
):
    by_core = [[2 * chip + core for chip in range(CHIPS)] for core in range(2)]
    swap_core = [(i, i ^ 1) for i in range(NT)]

    def across(x):
        moved = lax.all_to_all(x.reshape(CHIPS, CHUNK, 128), "tm", 0, 0, axis_index_groups=by_core)
        return moved.reshape(ROWS, 128)
    def blk_swap(x, bits):
        return lax.ppermute(x, "blk", [(i, i ^ bits) for i in range(8)])

    psi = psi_start.reshape(ROWS, 128)
    target = objective.reshape(ROWS, 128)
    faces = donor.reshape(4, 128)
    nearby = neighbours.reshape(ROWS, 128)
    match, slides = match_block.reshape(4), slide.reshape(4)
    sent = pack_donors(psi, faces)
    for sweep in range(SWEEPS):
        both = merge(MERGEHINTS[sweep], [sent, blk_swap(sent, 1)], [counts] if sweep == 0 else [])
        pieces = [both] + [blk_swap(both, 2 * hop) for hop in HOPS[1:]]
        states = across(psi)
        states, pieces[0] = lax.optimization_barrier((states, pieces[0]))
        coupling = across(couple(states, lax.ppermute(states, "tm", swap_core)))
        if sweep == LATE:
            pieces = [merge(BIGHINT, pieces[:3]), pieces[3]]
        residual, base = flux_part(FLUXHINTS[sweep], counts, match, slides, psi, nearby, target, jacobian[0, 0], pieces)
        if sweep == 0:
            dense, live, scale = prepare(counts, precond[0, 0], volume.reshape(GROUPS, 128), residual)
        more = [faces] if sweep + 1 < SWEEPS else []
        psi, *rest = finish(base, residual, coupling, live, scale, dense, *more)
        if rest:
            sent = rest[0]
    return psi.reshape(1, 1, F, CELLS)


def solution(mesh):
    in_specs = (
        P("tm", "blk", None, None),
        P("tm", "blk", None, None),
        P("tm", "blk", None, None, None, None),
        P("tm", "blk", None, None, None),
        P("blk", None),
        P("blk"),
        P("blk", None, None),
        P("blk", None),
        P("tm", "blk", None),
        P("tm", "blk", None),
    )
    out_specs = P("tm", "blk", None, None)
    return jax.shard_map(local, mesh=mesh, in_specs=in_specs, out_specs=out_specs, check_vma=False)
```

```python
import math

import numpy as np
import jax
import jax.numpy as jnp
from jax import lax
from jax.experimental import pallas as pl
from jax.experimental.pallas import tpu as pltpu
from jax.sharding import PartitionSpec as P

SWEEPS = 2
FLUXHINTS = (30000000000, 6000000)
MERGEHINTS = (65536, 65536)
LATE = 1
BIGHINT = 30000000000
F = 6
K = 6
CELLS = 8192
GROUPS = 64
STRIDE = 72
UNROLL = 16
HOPS = (0, 1, 3, 2)
ROWS = F * GROUPS
NT = 32
CHIPS = 16
CHUNK = ROWS // CHIPS
VMEM = pl.BlockSpec(memory_space=pltpu.VMEM)
SMEM = pl.BlockSpec(memory_space=pltpu.SMEM)
ANY = pl.BlockSpec(memory_space=pl.ANY)


def time_kernel():
    n = np.arange(NT)
    parity = np.where(n % 2 == 0, 1.0, -1.0)
    angle = np.where(n == 0, 0.5 * math.pi, math.pi * n / NT)
    sine = np.sin(angle)
    value = 0.5 * parity * np.cos(angle) / sine + 0.125 * parity / (sine * sine)
    return np.where(n == 0, 0.25 * (NT * NT + 2) / 12.0, value).astype(np.float32)


def params(mib=12):
    return pltpu.CompilerParams(vmem_limit_bytes=mib * 1024 * 1024)


def cost(flops, nbytes):
    return pl.CostEstimate(flops=flops, bytes_accessed=nbytes, transcendentals=0)


def f32_rows(n):
    return jax.ShapeDtypeStruct((n, 128), jnp.float32)


def i32_rows(n):
    return jax.ShapeDtypeStruct((n, 128), jnp.int32)


def lane_gather(data, index):
    return jnp.take_along_axis(data, index, axis=1, mode="promise_in_bounds")


def tile(start):
    return pl.ds(pl.multiple_of(start, 8), 8)


def fetch_donor_kernel(psi_hbm, donor_hbm, sent_ref, psi_ref, donor_ref, sems):
    copies = [pltpu.make_async_copy(donor_hbm, donor_ref, sems.at[F])]
    for f in range(F):
        rows = pl.ds(f * GROUPS, GROUPS // 2)
        copies.append(pltpu.make_async_copy(psi_hbm.at[rows, :], psi_ref.at[rows, :], sems.at[f]))
    for copy in copies:
        copy.start()
    for copy in copies:
        copy.wait()
    donor_kernel(psi_ref, donor_ref, sent_ref)


def donor_kernel(psi_ref, donor_ref, sent_ref):
    sublane = lax.broadcasted_iota(jnp.int32, (8, 128), 0)

    def block(q, carry):
        donor = jnp.broadcast_to(donor_ref[pl.ds(q, 1), :], (8, 128))
        lane = donor & 127
        home = (donor >> 7) - sublane
        rows = []
        for f in range(F):
            total = jnp.zeros((8, 128), jnp.float32)
            for b in range(4):
                picked = lane_gather(psi_ref[pl.ds(f * GROUPS + b * 8, 8), :], lane)
                total = total + jnp.where(home == b * 8, picked, 0.0)
            rows.append(jnp.sum(total, axis=0, keepdims=True))
        rows.append(jnp.zeros((2, 128), jnp.float32))
        sent_ref[tile(q * 8), :] = jnp.concatenate(rows, axis=0)
        return carry

    lax.fori_loop(0, 4, block, 0, unroll=2)


def pack_donors(psi, donor):
    return pl.pallas_call(
        fetch_donor_kernel,
        out_shape=f32_rows(32),
        in_specs=[ANY, ANY],
        out_specs=VMEM,
        scratch_shapes=[
            pltpu.VMEM((ROWS, 128), jnp.float32),
            pltpu.VMEM((4, 128), jnp.int32),
            pltpu.SemaphoreType.DMA((F + 1,)),
        ],
        compiler_params=params(50),
        cost_estimate=cost(30000000000, 220000),
        name="pack_donors",
    )(psi, donor)


def merge_kernel(*refs):
    height = refs[0].shape[0]
    for n in range(refs[-1].shape[0] // height):
        refs[-1][pl.ds(n * height, height), :] = refs[n][...]


def merge(hint, pieces, ready=()):
    return pl.pallas_call(
        merge_kernel,
        out_shape=f32_rows(sum(piece.shape[0] for piece in pieces)),
        in_specs=[VMEM] * len(pieces) + [ANY] * len(ready),
        out_specs=VMEM,
        compiler_params=params(),
        cost_estimate=cost(hint, 65536),
        name="merge",
    )(*pieces, *ready)


def prepare_kernel(counts_hbm, pre_hbm, volume_hbm, after_ref, dense_ref, live_ref, scale_ref, pre_ref, volume_ref, counts_ref, sems):
    copies = [
        pltpu.make_async_copy(counts_hbm, counts_ref, sems.at[0]),
        pltpu.make_async_copy(volume_hbm, volume_ref, sems.at[1]),
        pltpu.make_async_copy(pre_hbm, pre_ref, sems.at[2]),
    ]
    for copy in copies:
        copy.start()
    copies[0].wait()
    copies[1].wait()
    for b in range(8):
        live = live_rows(counts_ref, b)
        live_ref[pl.ds(b * 8, 8), :] = live
        scale_ref[pl.ds(b * 8, 8), :] = live * volume_ref[pl.ds(b * 8, 8), :]
    copies[2].wait()

    def step(g, carry):
        at = pl.multiple_of(g * 128, 128)
        for i in range(F):
            dense_ref[pl.ds(i * F * STRIDE + g, F, stride=STRIDE), :] = pre_ref[i, :, pl.ds(at, 128)].astype(jnp.float32)
        return carry

    lax.fori_loop(0, GROUPS, step, 0, unroll=8)


def prepare(counts, precond, volume, after):
    return pl.pallas_call(
        prepare_kernel,
        out_shape=(f32_rows(F * F * STRIDE), f32_rows(GROUPS), f32_rows(GROUPS)),
        in_specs=[ANY] * 4,
        out_specs=(VMEM,) * 3,
        scratch_shapes=[
            pltpu.VMEM((F, F, CELLS), jnp.bfloat16),
            pltpu.VMEM((GROUPS, 128), jnp.float32),
            pltpu.SMEM((1,), jnp.int32),
            pltpu.SemaphoreType.DMA((3,)),
        ],
        compiler_params=params(50),
        cost_estimate=cost(1000000, 2500000),
        name="prepare",
    )(counts, precond, volume, after)


def live_rows(counts_ref, block):
    cell = lax.broadcasted_iota(jnp.int32, (8, 128), 0) * 128 + lax.broadcasted_iota(jnp.int32, (8, 128), 1)
    return jnp.where(cell + block * 1024 < counts_ref[0], 1.0, 0.0)


def flux_kernel(
    counts_hbm, match_hbm, slide_hbm, psi_hbm, nbr_hbm, target_hbm, jac_hbm, *refs
):
    pieces = refs[:-13]
    (out_ref, psi_s, counts_ref, match_ref, slide_ref, nbr_s, target_s, jac_s, stencil_s, pool_s, ghost_s, part_s, sems) = refs[-13:]
    small = [
        pltpu.make_async_copy(counts_hbm, counts_ref, sems.at[8]),
        pltpu.make_async_copy(match_hbm, match_ref, sems.at[9]),
        pltpu.make_async_copy(slide_hbm, slide_ref, sems.at[10]),
    ]
    nbr_copy = pltpu.make_async_copy(nbr_hbm, nbr_s, sems.at[11])
    psi_copy = pltpu.make_async_copy(psi_hbm, psi_s, sems.at[12])
    target_copy = pltpu.make_async_copy(target_hbm, target_s, sems.at[13])

    def jac_copy(b):
        cells = pl.ds(pl.multiple_of(b * 1024, 1024), 1024)
        return pltpu.make_async_copy(jac_hbm.at[:, :, :, cells], jac_s.at[:, :, :, cells], sems.at[b])

    for copy in small:
        copy.start()
    nbr_copy.start()
    psi_copy.start()
    for b in range(8):
        jac_copy(b).start()
    target_copy.start()
    hops = iter(HOPS)
    for piece in pieces:
        for n in range(piece.shape[0] // 64):
            pool_s[pl.ds(next(hops) * 64, 64), :] = piece[pl.ds(n * 64, 64), :]
    stencil_s[...] = jnp.zeros_like(stencil_s)
    own = lax.axis_index("blk")
    lane = lax.broadcasted_iota(jnp.int32, (8, 128), 1)
    for copy in small:
        copy.wait()
    for q in range(4):
        block = match_ref[q]
        part = block // 4
        hop = (part // 2) ^ (own // 2)
        side = lax.rem(part, 2) ^ lax.rem(own, 2)
        source = pool_s[tile((hop * 8 + side * 4 + lax.rem(block, 4)) * 8), :]
        ghost_s[pl.ds(q * 8, 8), :] = lane_gather(source, (lane + slide_ref[q]) & 127)
    nbr_copy.wait()
    for k in range(K):
        for b in range(8):
            stencil_s[pl.ds(b * 64 + k, 8, stride=8), :] = nbr_s[pl.ds(k * GROUPS + b * 8, 8), :]
    psi_copy.wait()
    for b in range(8):
        live = live_rows(counts_ref, b)
        for f in range(F):
            rows = pl.ds(f * GROUPS + b * 8, 8)
            psi_s[rows, :] = psi_s[rows, :] * live

    def step(b, carry):
        for n in range(UNROLL // 8):
            jac_copy(b * (UNROLL // 8) + n).wait()
        for s in range(UNROLL):
            g = b * UNROLL + s
            at = pl.multiple_of(g * 128, 128)
            index = stencil_s[tile(g * 8), :]
            outside = index >= 128
            pick = index & 127
            total = [None] * F
            for j in range(F):
                inner = jnp.broadcast_to(psi_s[pl.ds(j * GROUPS + g, 1), :], (8, 128))
                outer = jnp.broadcast_to(ghost_s[pl.ds((s % 4) * 8 + j, 1), :], (8, 128))
                value = jnp.where(outside, lane_gather(outer, pick), lane_gather(inner, pick))[:K]
                for i in range(F):
                    term = jac_s[i, j, :, pl.ds(at, 128)].astype(jnp.float32) * value
                    total[i] = term if j == 0 else total[i] + term
            for i in range(F):
                part_s[pl.ds(pl.multiple_of(g * 48 + i * 8, 8), K), :] = total[i]
        return carry

    lax.fori_loop(0, GROUPS // UNROLL, step, 0)
    target_copy.wait()

    def gather_up(b, carry):
        for j in range(F):
            flux = part_s[pl.ds(b * 384 + j * 8, 8, stride=48), :]
            for k in range(1, K):
                flux = flux + part_s[pl.ds(b * 384 + j * 8 + k, 8, stride=48), :]
            rows = tile(j * GROUPS + b * 8)
            out_ref[rows, :] = flux - target_s[rows, :]
        return carry

    lax.fori_loop(0, 8, gather_up, 0, unroll=2)


def flux_part(hint, counts, match, slide, psi, neighbours, target, jac, pieces):
    return pl.pallas_call(
        flux_kernel,
        out_shape=(f32_rows(ROWS), f32_rows(ROWS)),
        in_specs=[ANY] * 7 + [VMEM] * len(pieces),
        out_specs=(VMEM, VMEM),
        scratch_shapes=[
            pltpu.SMEM((1,), jnp.int32),
            pltpu.SMEM((4,), jnp.int32),
            pltpu.SMEM((4,), jnp.int32),
            pltpu.VMEM((ROWS, 128), jnp.int32),
            pltpu.VMEM((ROWS, 128), jnp.float32),
            pltpu.VMEM((F, F, K, CELLS), jnp.bfloat16),
            pltpu.VMEM((GROUPS * 8, 128), jnp.int32),
            pltpu.VMEM((256, 128), jnp.float32),
            pltpu.VMEM((32, 128), jnp.float32),
            pltpu.VMEM((GROUPS * 48, 128), jnp.float32),
            pltpu.SemaphoreType.DMA((14,)),
        ],
        compiler_params=params(50),
        cost_estimate=cost(hint, 7000000),
        name="flux_part",
    )(counts, match, slide, psi, neighbours, target, jac, *pieces)


def couple_kernel(own_ref, other_ref, out_hbm, out_ref, sems):
    def put(n):
        rows = pl.ds(n * 8 * CHUNK, 8 * CHUNK)
        return pltpu.make_async_copy(out_ref.at[rows, :], out_hbm.at[rows, :], sems.at[n])

    f = [float(v) for v in time_kernel()]
    first = lax.rem(lax.axis_index("tm"), 2) == 0
    even = f[0::2]
    odd = [jnp.where(first, f[2 * n + 1], f[2 * n - 1]) for n in range(CHIPS)]
    for t0 in range(0, CHIPS, 8):
        for r in range(CHUNK // 8):
            total = [None] * 8
            for s in range(CHIPS):
                own = own_ref[pl.ds(s * CHUNK + r * 8, 8), :]
                other = other_ref[pl.ds(s * CHUNK + r * 8, 8), :]
                for t in range(8):
                    n = (s - t0 - t) % CHIPS
                    term = even[n] * own + odd[n] * other
                    total[t] = term if s == 0 else total[t] + term
            for t in range(8):
                out_ref[pl.ds((t0 + t) * CHUNK + r * 8, 8), :] = total[t]
        put(t0 // 8).start()
    for n in range(2):
        put(n).wait()


def couple(own, other):
    return pl.pallas_call(
        couple_kernel,
        out_shape=f32_rows(ROWS),
        in_specs=[VMEM, VMEM],
        out_specs=ANY,
        scratch_shapes=[pltpu.VMEM((ROWS, 128), jnp.float32), pltpu.SemaphoreType.DMA((2,))],
        compiler_params=params(),
        cost_estimate=cost(3200000, 600000),
        name="couple",
    )(own, other)


def finish_kernel(base_ref, residual_ref, coupling_ref, live_ref, scale_ref, dense_ref, *rest):
    out_hbm = rest[-3] if len(rest) == 3 else rest[1]
    out_ref, sems = rest[-2:]

    def put(half, f):
        rows = pl.ds(f * GROUPS + half * 32, 32)
        return pltpu.make_async_copy(out_ref.at[rows, :], out_hbm.at[rows, :], sems.at[half * F + f])

    def step(b, carry):
        live = live_ref[tile(b * 8), :]
        scale = scale_ref[tile(b * 8), :]
        whole = []
        for j in range(F):
            rows = tile(j * GROUPS + b * 8)
            whole.append(live * residual_ref[rows, :] + scale * coupling_ref[rows, :])
        for i in range(F):
            rows = tile(i * GROUPS + b * 8)
            value = base_ref[rows, :]
            for j in range(F):
                value = value - dense_ref[tile((i * F + j) * STRIDE + b * 8), :] * whole[j]
            out_ref[rows, :] = value
        return carry

    for half in range(2):
        lax.fori_loop(half * 4, half * 4 + 4, step, 0)
        for f in range(F):
            put(half, f).start()
    if len(rest) > 3:
        donor_kernel(out_ref, rest[0], rest[2])
    for half in range(2):
        for f in range(F):
            put(half, f).wait()


def finish(base, residual, coupling, live, scale, dense, donor=None):
    operands = [base, residual, coupling, live, scale, dense] + ([] if donor is None else [donor])
    shapes = [f32_rows(ROWS)] + ([] if donor is None else [f32_rows(32)])
    return pl.pallas_call(
        finish_kernel,
        out_shape=shapes,
        in_specs=[VMEM] * len(operands),
        out_specs=[ANY, VMEM][: len(shapes)],
        scratch_shapes=[pltpu.VMEM((ROWS, 128), jnp.float32), pltpu.SemaphoreType.DMA((2 * F,))],
        compiler_params=params(),
        cost_estimate=cost(600000, 2000000),
        name="finish",
    )(*operands)


def local(
    psi_start, objective, jacobian, precond, volume, counts, neighbours, donor, match_block, slide
):
    by_core = [[2 * chip + core for chip in range(CHIPS)] for core in range(2)]
    swap_core = [(i, i ^ 1) for i in range(NT)]

    def across(x):
        moved = lax.all_to_all(x.reshape(CHIPS, CHUNK, 128), "tm", 0, 0, axis_index_groups=by_core)
        return moved.reshape(ROWS, 128)
    def blk_swap(x, bits):
        return lax.ppermute(x, "blk", [(i, i ^ bits) for i in range(8)])

    psi = psi_start.reshape(ROWS, 128)
    target = objective.reshape(ROWS, 128)
    faces = donor.reshape(4, 128)
    nearby = neighbours.reshape(ROWS, 128)
    match, slides = match_block.reshape(4), slide.reshape(4)
    sent = pack_donors(psi, faces)
    for sweep in range(SWEEPS):
        both = merge(MERGEHINTS[sweep], [sent, blk_swap(sent, 1)], [counts] if sweep == 0 else [])
        pieces = [both] + [blk_swap(both, 2 * hop) for hop in HOPS[1:]]
        if sweep == 0:
            psi, sent = lax.optimization_barrier((psi, sent))
        states = across(psi)
        states, pieces[0] = lax.optimization_barrier((states, pieces[0]))
        coupling = across(couple(states, lax.ppermute(states, "tm", swap_core)))
        if sweep == LATE:
            pieces = [merge(BIGHINT, pieces[:3]), pieces[3]]
        residual, base = flux_part(FLUXHINTS[sweep], counts, match, slides, psi, nearby, target, jacobian[0, 0], pieces)
        if sweep == 0:
            dense, live, scale = prepare(counts, precond[0, 0], volume.reshape(GROUPS, 128), residual)
        more = [faces] if sweep + 1 < SWEEPS else []
        psi, *rest = finish(base, residual, coupling, live, scale, dense, *more)
        if rest:
            sent = rest[0]
    return psi.reshape(1, 1, F, CELLS)


def solution(mesh):
    in_specs = (
        P("tm", "blk", None, None),
        P("tm", "blk", None, None),
        P("tm", "blk", None, None, None, None),
        P("tm", "blk", None, None, None),
        P("blk", None),
        P("blk"),
        P("blk", None, None),
        P("blk", None),
        P("tm", "blk", None),
        P("tm", "blk", None),
    )
    out_specs = P("tm", "blk", None, None)
    return jax.shard_map(local, mesh=mesh, in_specs=in_specs, out_specs=out_specs, check_vma=False)
```

```python
import math

import numpy as np
import jax
import jax.numpy as jnp
from jax import lax
from jax.experimental import pallas as pl
from jax.experimental.pallas import tpu as pltpu
from jax.sharding import PartitionSpec as P

SWEEPS = 2
FLUXHINTS = (30000000000, 30000000000)
MERGEHINTS = (65536, 65536)
F = 6
K = 6
CELLS = 8192
GROUPS = 64
STRIDE = 72
UNROLL = 16
HOPS = (0, 1, 2, 3)
ROWS = F * GROUPS
NT = 32
CHIPS = 16
CHUNK = ROWS // CHIPS
VMEM = pl.BlockSpec(memory_space=pltpu.VMEM)
SMEM = pl.BlockSpec(memory_space=pltpu.SMEM)
ANY = pl.BlockSpec(memory_space=pl.ANY)


def time_kernel():
    n = np.arange(NT)
    parity = np.where(n % 2 == 0, 1.0, -1.0)
    angle = np.where(n == 0, 0.5 * math.pi, math.pi * n / NT)
    sine = np.sin(angle)
    value = 0.5 * parity * np.cos(angle) / sine + 0.125 * parity / (sine * sine)
    return np.where(n == 0, 0.25 * (NT * NT + 2) / 12.0, value).astype(np.float32)


def params(mib=12):
    return pltpu.CompilerParams(vmem_limit_bytes=mib * 1024 * 1024)


def cost(flops, nbytes):
    return pl.CostEstimate(flops=flops, bytes_accessed=nbytes, transcendentals=0)


def f32_rows(n):
    return jax.ShapeDtypeStruct((n, 128), jnp.float32)


def i32_rows(n):
    return jax.ShapeDtypeStruct((n, 128), jnp.int32)


def lane_gather(data, index):
    return jnp.take_along_axis(data, index, axis=1, mode="promise_in_bounds")


def tile(start):
    return pl.ds(pl.multiple_of(start, 8), 8)


def fetch_donor_kernel(psi_hbm, donor_hbm, sent_ref, psi_ref, donor_ref, sems):
    copies = [pltpu.make_async_copy(donor_hbm, donor_ref, sems.at[F])]
    for f in range(F):
        rows = pl.ds(f * GROUPS, GROUPS // 2)
        copies.append(pltpu.make_async_copy(psi_hbm.at[rows, :], psi_ref.at[rows, :], sems.at[f]))
    for copy in copies:
        copy.start()
    for copy in copies:
        copy.wait()
    donor_kernel(psi_ref, donor_ref, sent_ref)


def donor_kernel(psi_ref, donor_ref, sent_ref):
    sublane = lax.broadcasted_iota(jnp.int32, (8, 128), 0)

    def block(q, carry):
        donor = jnp.broadcast_to(donor_ref[pl.ds(q, 1), :], (8, 128))
        lane = donor & 127
        home = (donor >> 7) - sublane
        rows = []
        for f in range(F):
            total = jnp.zeros((8, 128), jnp.float32)
            for b in range(4):
                picked = lane_gather(psi_ref[pl.ds(f * GROUPS + b * 8, 8), :], lane)
                total = total + jnp.where(home == b * 8, picked, 0.0)
            rows.append(jnp.sum(total, axis=0, keepdims=True))
        rows.append(jnp.zeros((2, 128), jnp.float32))
        sent_ref[tile(q * 8), :] = jnp.concatenate(rows, axis=0)
        return carry

    lax.fori_loop(0, 4, block, 0, unroll=2)


def pack_donors(psi, donor):
    return pl.pallas_call(
        fetch_donor_kernel,
        out_shape=f32_rows(32),
        in_specs=[ANY, ANY],
        out_specs=VMEM,
        scratch_shapes=[
            pltpu.VMEM((ROWS, 128), jnp.float32),
            pltpu.VMEM((4, 128), jnp.int32),
            pltpu.SemaphoreType.DMA((F + 1,)),
        ],
        compiler_params=params(50),
        cost_estimate=cost(30000000000, 220000),
        name="pack_donors",
    )(psi, donor)


def merge_kernel(*refs):
    height = refs[0].shape[0]
    for n in range(refs[-1].shape[0] // height):
        refs[-1][pl.ds(n * height, height), :] = refs[n][...]


def merge(hint, pieces, ready=()):
    return pl.pallas_call(
        merge_kernel,
        out_shape=f32_rows(sum(piece.shape[0] for piece in pieces)),
        in_specs=[VMEM] * len(pieces) + [ANY] * len(ready),
        out_specs=VMEM,
        compiler_params=params(),
        cost_estimate=cost(hint, 65536),
        name="merge",
    )(*pieces, *ready)


def prepare_kernel(counts_hbm, pre_hbm, volume_hbm, after_ref, dense_ref, live_ref, scale_ref, pre_ref, volume_ref, counts_ref, sems):
    copies = [
        pltpu.make_async_copy(counts_hbm, counts_ref, sems.at[0]),
        pltpu.make_async_copy(volume_hbm, volume_ref, sems.at[1]),
        pltpu.make_async_copy(pre_hbm, pre_ref, sems.at[2]),
    ]
    for copy in copies:
        copy.start()
    copies[0].wait()
    copies[1].wait()
    for b in range(8):
        live = live_rows(counts_ref, b)
        live_ref[pl.ds(b * 8, 8), :] = live
        scale_ref[pl.ds(b * 8, 8), :] = live * volume_ref[pl.ds(b * 8, 8), :]
    copies[2].wait()

    def step(g, carry):
        at = pl.multiple_of(g * 128, 128)
        for i in range(F):
            dense_ref[pl.ds(i * F * STRIDE + g, F, stride=STRIDE), :] = pre_ref[i, :, pl.ds(at, 128)].astype(jnp.float32)
        return carry

    lax.fori_loop(0, GROUPS, step, 0, unroll=8)


def prepare(counts, precond, volume, after):
    return pl.pallas_call(
        prepare_kernel,
        out_shape=(f32_rows(F * F * STRIDE), f32_rows(GROUPS), f32_rows(GROUPS)),
        in_specs=[ANY] * 4,
        out_specs=(VMEM,) * 3,
        scratch_shapes=[
            pltpu.VMEM((F, F, CELLS), jnp.bfloat16),
            pltpu.VMEM((GROUPS, 128), jnp.float32),
            pltpu.SMEM((1,), jnp.int32),
            pltpu.SemaphoreType.DMA((3,)),
        ],
        compiler_params=params(50),
        cost_estimate=cost(1000000, 2500000),
        name="prepare",
    )(counts, precond, volume, after)


def live_rows(counts_ref, block):
    cell = lax.broadcasted_iota(jnp.int32, (8, 128), 0) * 128 + lax.broadcasted_iota(jnp.int32, (8, 128), 1)
    return jnp.where(cell + block * 1024 < counts_ref[0], 1.0, 0.0)


def flux_kernel(
    counts_hbm, match_hbm, slide_hbm, psi_hbm, nbr_hbm, target_hbm, jac_hbm, *refs
):
    pieces = refs[:-13]
    (out_ref, psi_s, counts_ref, match_ref, slide_ref, nbr_s, target_s, jac_s, stencil_s, pool_s, ghost_s, part_s, sems) = refs[-13:]
    small = [
        pltpu.make_async_copy(counts_hbm, counts_ref, sems.at[8]),
        pltpu.make_async_copy(match_hbm, match_ref, sems.at[9]),
        pltpu.make_async_copy(slide_hbm, slide_ref, sems.at[10]),
    ]
    nbr_copy = pltpu.make_async_copy(nbr_hbm, nbr_s, sems.at[11])
    psi_copy = pltpu.make_async_copy(psi_hbm, psi_s, sems.at[12])
    target_copy = pltpu.make_async_copy(target_hbm, target_s, sems.at[13])

    def jac_copy(b):
        cells = pl.ds(pl.multiple_of(b * 1024, 1024), 1024)
        return pltpu.make_async_copy(jac_hbm.at[:, :, :, cells], jac_s.at[:, :, :, cells], sems.at[b])

    for copy in small:
        copy.start()
    nbr_copy.start()
    psi_copy.start()
    for b in range(8):
        jac_copy(b).start()
    target_copy.start()
    hops = iter(HOPS)
    for piece in pieces:
        for n in range(piece.shape[0] // 64):
            pool_s[pl.ds(next(hops) * 64, 64), :] = piece[pl.ds(n * 64, 64), :]
    stencil_s[...] = jnp.zeros_like(stencil_s)
    own = lax.axis_index("blk")
    lane = lax.broadcasted_iota(jnp.int32, (8, 128), 1)
    for copy in small:
        copy.wait()
    for q in range(4):
        block = match_ref[q]
        part = block // 4
        hop = (part // 2) ^ (own // 2)
        side = lax.rem(part, 2) ^ lax.rem(own, 2)
        source = pool_s[tile((hop * 8 + side * 4 + lax.rem(block, 4)) * 8), :]
        ghost_s[pl.ds(q * 8, 8), :] = lane_gather(source, (lane + slide_ref[q]) & 127)
    nbr_copy.wait()
    for k in range(K):
        for b in range(8):
            stencil_s[pl.ds(b * 64 + k, 8, stride=8), :] = nbr_s[pl.ds(k * GROUPS + b * 8, 8), :]
    psi_copy.wait()
    for b in range(8):
        live = live_rows(counts_ref, b)
        for f in range(F):
            rows = pl.ds(f * GROUPS + b * 8, 8)
            psi_s[rows, :] = psi_s[rows, :] * live

    def step(b, carry):
        for n in range(UNROLL // 8):
            jac_copy(b * (UNROLL // 8) + n).wait()
        for s in range(UNROLL):
            g = b * UNROLL + s
            at = pl.multiple_of(g * 128, 128)
            index = stencil_s[tile(g * 8), :]
            outside = index >= 128
            pick = index & 127
            total = [None] * F
            for j in range(F):
                inner = jnp.broadcast_to(psi_s[pl.ds(j * GROUPS + g, 1), :], (8, 128))
                outer = jnp.broadcast_to(ghost_s[pl.ds((s % 4) * 8 + j, 1), :], (8, 128))
                value = jnp.where(outside, lane_gather(outer, pick), lane_gather(inner, pick))[:K]
                for i in range(F):
                    term = jac_s[i, j, :, pl.ds(at, 128)].astype(jnp.float32) * value
                    total[i] = term if j == 0 else total[i] + term
            for i in range(F):
                part_s[pl.ds(pl.multiple_of(g * 48 + i * 8, 8), K), :] = total[i]
        return carry

    lax.fori_loop(0, GROUPS // UNROLL, step, 0)
    target_copy.wait()

    def gather_up(b, carry):
        for j in range(F):
            flux = part_s[pl.ds(b * 384 + j * 8, 8, stride=48), :]
            for k in range(1, K):
                flux = flux + part_s[pl.ds(b * 384 + j * 8 + k, 8, stride=48), :]
            rows = tile(j * GROUPS + b * 8)
            out_ref[rows, :] = flux - target_s[rows, :]
        return carry

    lax.fori_loop(0, 8, gather_up, 0, unroll=2)


def flux_part(hint, counts, match, slide, psi, neighbours, target, jac, pieces):
    return pl.pallas_call(
        flux_kernel,
        out_shape=(f32_rows(ROWS), f32_rows(ROWS)),
        in_specs=[ANY] * 7 + [VMEM] * len(pieces),
        out_specs=(VMEM, VMEM),
        scratch_shapes=[
            pltpu.SMEM((1,), jnp.int32),
            pltpu.SMEM((4,), jnp.int32),
            pltpu.SMEM((4,), jnp.int32),
            pltpu.VMEM((ROWS, 128), jnp.int32),
            pltpu.VMEM((ROWS, 128), jnp.float32),
            pltpu.VMEM((F, F, K, CELLS), jnp.bfloat16),
            pltpu.VMEM((GROUPS * 8, 128), jnp.int32),
            pltpu.VMEM((256, 128), jnp.float32),
            pltpu.VMEM((32, 128), jnp.float32),
            pltpu.VMEM((GROUPS * 48, 128), jnp.float32),
            pltpu.SemaphoreType.DMA((14,)),
        ],
        compiler_params=params(50),
        cost_estimate=cost(hint, 7000000),
        name="flux_part",
    )(counts, match, slide, psi, neighbours, target, jac, *pieces)


def couple_kernel(own_ref, other_ref, out_hbm, out_ref, sems):
    def put(n):
        rows = pl.ds(n * 8 * CHUNK, 8 * CHUNK)
        return pltpu.make_async_copy(out_ref.at[rows, :], out_hbm.at[rows, :], sems.at[n])

    f = [float(v) for v in time_kernel()]
    first = lax.rem(lax.axis_index("tm"), 2) == 0
    even = f[0::2]
    odd = [jnp.where(first, f[2 * n + 1], f[2 * n - 1]) for n in range(CHIPS)]
    for t0 in range(0, CHIPS, 8):
        for r in range(CHUNK // 8):
            total = [None] * 8
            for s in range(CHIPS):
                own = own_ref[pl.ds(s * CHUNK + r * 8, 8), :]
                other = other_ref[pl.ds(s * CHUNK + r * 8, 8), :]
                for t in range(8):
                    n = (s - t0 - t) % CHIPS
                    term = even[n] * own + odd[n] * other
                    total[t] = term if s == 0 else total[t] + term
            for t in range(8):
                out_ref[pl.ds((t0 + t) * CHUNK + r * 8, 8), :] = total[t]
        put(t0 // 8).start()
    for n in range(2):
        put(n).wait()


def couple(own, other):
    return pl.pallas_call(
        couple_kernel,
        out_shape=f32_rows(ROWS),
        in_specs=[VMEM, VMEM],
        out_specs=ANY,
        scratch_shapes=[pltpu.VMEM((ROWS, 128), jnp.float32), pltpu.SemaphoreType.DMA((2,))],
        compiler_params=params(),
        cost_estimate=cost(3200000, 600000),
        name="couple",
    )(own, other)


def finish_kernel(base_ref, residual_ref, coupling_ref, live_ref, scale_ref, dense_ref, *rest):
    out_hbm = rest[-3] if len(rest) == 3 else rest[1]
    out_ref, sems = rest[-2:]

    def put(half, f):
        rows = pl.ds(f * GROUPS + half * 32, 32)
        return pltpu.make_async_copy(out_ref.at[rows, :], out_hbm.at[rows, :], sems.at[half * F + f])

    def step(b, carry):
        live = live_ref[tile(b * 8), :]
        scale = scale_ref[tile(b * 8), :]
        whole = []
        for j in range(F):
            rows = tile(j * GROUPS + b * 8)
            whole.append(live * residual_ref[rows, :] + scale * coupling_ref[rows, :])
        for i in range(F):
            rows = tile(i * GROUPS + b * 8)
            value = base_ref[rows, :]
            for j in range(F):
                value = value - dense_ref[tile((i * F + j) * STRIDE + b * 8), :] * whole[j]
            out_ref[rows, :] = value
        return carry

    for half in range(2):
        lax.fori_loop(half * 4, half * 4 + 4, step, 0)
        for f in range(F):
            put(half, f).start()
    if len(rest) > 3:
        donor_kernel(out_ref, rest[0], rest[2])
    for half in range(2):
        for f in range(F):
            put(half, f).wait()


def finish(base, residual, coupling, live, scale, dense, donor=None):
    operands = [base, residual, coupling, live, scale, dense] + ([] if donor is None else [donor])
    shapes = [f32_rows(ROWS)] + ([] if donor is None else [f32_rows(32)])
    return pl.pallas_call(
        finish_kernel,
        out_shape=shapes,
        in_specs=[VMEM] * len(operands),
        out_specs=[ANY, VMEM][: len(shapes)],
        scratch_shapes=[pltpu.VMEM((ROWS, 128), jnp.float32), pltpu.SemaphoreType.DMA((2 * F,))],
        compiler_params=params(),
        cost_estimate=cost(600000, 2000000),
        name="finish",
    )(*operands)


def local(
    psi_start, objective, jacobian, precond, volume, counts, neighbours, donor, match_block, slide
):
    by_core = [[2 * chip + core for chip in range(CHIPS)] for core in range(2)]
    swap_core = [(i, i ^ 1) for i in range(NT)]

    def across(x):
        moved = lax.all_to_all(x.reshape(CHIPS, CHUNK, 128), "tm", 0, 0, axis_index_groups=by_core)
        return moved.reshape(ROWS, 128)
    def blk_swap(x, bits):
        return lax.ppermute(x, "blk", [(i, i ^ bits) for i in range(8)])

    psi = psi_start.reshape(ROWS, 128)
    target = objective.reshape(ROWS, 128)
    faces = donor.reshape(4, 128)
    nearby = neighbours.reshape(ROWS, 128)
    match, slides = match_block.reshape(4), slide.reshape(4)
    sent = pack_donors(psi, faces)
    for sweep in range(SWEEPS):
        both = merge(MERGEHINTS[sweep], [sent, blk_swap(sent, 1)], [counts] if sweep == 0 else [])
        pieces = [both] + [blk_swap(both, 2 * hop) for hop in HOPS[1:]]
        if sweep == 0:
            psi, sent = lax.optimization_barrier((psi, sent))
        states = across(psi)
        states, pieces[0] = lax.optimization_barrier((states, pieces[0]))
        coupling = across(couple(states, lax.ppermute(states, "tm", swap_core)))
        residual, base = flux_part(FLUXHINTS[sweep], counts, match, slides, psi, nearby, target, jacobian[0, 0], pieces)
        if sweep == 0:
            dense, live, scale = prepare(counts, precond[0, 0], volume.reshape(GROUPS, 128), residual)
        more = [faces] if sweep + 1 < SWEEPS else []
        psi, *rest = finish(base, residual, coupling, live, scale, dense, *more)
        if rest:
            sent = rest[0]
    return psi.reshape(1, 1, F, CELLS)


def solution(mesh):
    in_specs = (
        P("tm", "blk", None, None),
        P("tm", "blk", None, None),
        P("tm", "blk", None, None, None, None),
        P("tm", "blk", None, None, None),
        P("blk", None),
        P("blk"),
        P("blk", None, None),
        P("blk", None),
        P("tm", "blk", None),
        P("tm", "blk", None),
    )
    out_specs = P("tm", "blk", None, None)
    return jax.shard_map(local, mesh=mesh, in_specs=in_specs, out_specs=out_specs, check_vma=False)
```

```python
import math

import numpy as np
import jax
import jax.numpy as jnp
from jax import lax
from jax.experimental import pallas as pl
from jax.experimental.pallas import tpu as pltpu
from jax.sharding import PartitionSpec as P

SWEEPS = 2
FLUXHINTS = (30000000000, 30000000000)
MERGEHINTS = (65536, 65536)
F = 6
K = 6
CELLS = 8192
GROUPS = 64
STRIDE = 72
UNROLL = 16
HOPS = (0, 1, 2, 3)
ROWS = F * GROUPS
NT = 32
CHIPS = 16
CHUNK = ROWS // CHIPS
VMEM = pl.BlockSpec(memory_space=pltpu.VMEM)
SMEM = pl.BlockSpec(memory_space=pltpu.SMEM)
ANY = pl.BlockSpec(memory_space=pl.ANY)


def time_kernel():
    n = np.arange(NT)
    parity = np.where(n % 2 == 0, 1.0, -1.0)
    angle = np.where(n == 0, 0.5 * math.pi, math.pi * n / NT)
    sine = np.sin(angle)
    value = 0.5 * parity * np.cos(angle) / sine + 0.125 * parity / (sine * sine)
    return np.where(n == 0, 0.25 * (NT * NT + 2) / 12.0, value).astype(np.float32)


def params(mib=12):
    return pltpu.CompilerParams(vmem_limit_bytes=mib * 1024 * 1024)


def cost(flops, nbytes):
    return pl.CostEstimate(flops=flops, bytes_accessed=nbytes, transcendentals=0)


def f32_rows(n):
    return jax.ShapeDtypeStruct((n, 128), jnp.float32)


def i32_rows(n):
    return jax.ShapeDtypeStruct((n, 128), jnp.int32)


def lane_gather(data, index):
    return jnp.take_along_axis(data, index, axis=1, mode="promise_in_bounds")


def tile(start):
    return pl.ds(pl.multiple_of(start, 8), 8)


def fetch_donor_kernel(psi_hbm, donor_hbm, sent_ref, psi_ref, donor_ref, sems):
    copies = [pltpu.make_async_copy(donor_hbm, donor_ref, sems.at[F])]
    for f in range(F):
        rows = pl.ds(f * GROUPS, GROUPS // 2)
        copies.append(pltpu.make_async_copy(psi_hbm.at[rows, :], psi_ref.at[rows, :], sems.at[f]))
    for copy in copies:
        copy.start()
    for copy in copies:
        copy.wait()
    donor_kernel(psi_ref, donor_ref, sent_ref)


def donor_kernel(psi_ref, donor_ref, sent_ref):
    sublane = lax.broadcasted_iota(jnp.int32, (8, 128), 0)

    def block(q, carry):
        donor = jnp.broadcast_to(donor_ref[pl.ds(q, 1), :], (8, 128))
        lane = donor & 127
        home = (donor >> 7) - sublane
        rows = []
        for f in range(F):
            total = jnp.zeros((8, 128), jnp.float32)
            for b in range(4):
                picked = lane_gather(psi_ref[pl.ds(f * GROUPS + b * 8, 8), :], lane)
                total = total + jnp.where(home == b * 8, picked, 0.0)
            rows.append(jnp.sum(total, axis=0, keepdims=True))
        rows.append(jnp.zeros((2, 128), jnp.float32))
        sent_ref[tile(q * 8), :] = jnp.concatenate(rows, axis=0)
        return carry

    lax.fori_loop(0, 4, block, 0, unroll=2)


def pack_donors(psi, donor):
    return pl.pallas_call(
        fetch_donor_kernel,
        out_shape=f32_rows(32),
        in_specs=[ANY, ANY],
        out_specs=VMEM,
        scratch_shapes=[
            pltpu.VMEM((ROWS, 128), jnp.float32),
            pltpu.VMEM((4, 128), jnp.int32),
            pltpu.SemaphoreType.DMA((F + 1,)),
        ],
        compiler_params=params(50),
        cost_estimate=cost(30000000000, 220000),
        name="pack_donors",
    )(psi, donor)


def merge_kernel(*refs):
    height = refs[0].shape[0]
    for n in range(refs[-1].shape[0] // height):
        refs[-1][pl.ds(n * height, height), :] = refs[n][...]


def merge(hint, pieces, ready=()):
    return pl.pallas_call(
        merge_kernel,
        out_shape=f32_rows(sum(piece.shape[0] for piece in pieces)),
        in_specs=[VMEM] * len(pieces) + [ANY] * len(ready),
        out_specs=VMEM,
        compiler_params=params(),
        cost_estimate=cost(hint, 65536),
        name="merge",
    )(*pieces, *ready)


def prepare_kernel(counts_hbm, pre_hbm, volume_hbm, after_ref, dense_ref, live_ref, scale_ref, pre_ref, volume_ref, counts_ref, sems):
    copies = [
        pltpu.make_async_copy(counts_hbm, counts_ref, sems.at[0]),
        pltpu.make_async_copy(volume_hbm, volume_ref, sems.at[1]),
        pltpu.make_async_copy(pre_hbm, pre_ref, sems.at[2]),
    ]
    for copy in copies:
        copy.start()
    copies[0].wait()
    copies[1].wait()
    for b in range(8):
        live = live_rows(counts_ref, b)
        live_ref[pl.ds(b * 8, 8), :] = live
        scale_ref[pl.ds(b * 8, 8), :] = live * volume_ref[pl.ds(b * 8, 8), :]
    copies[2].wait()

    def step(g, carry):
        at = pl.multiple_of(g * 128, 128)
        for i in range(F):
            dense_ref[pl.ds(i * F * STRIDE + g, F, stride=STRIDE), :] = pre_ref[i, :, pl.ds(at, 128)].astype(jnp.float32)
        return carry

    lax.fori_loop(0, GROUPS, step, 0, unroll=8)


def prepare(counts, precond, volume, after):
    return pl.pallas_call(
        prepare_kernel,
        out_shape=(f32_rows(F * F * STRIDE), f32_rows(GROUPS), f32_rows(GROUPS)),
        in_specs=[ANY] * 4,
        out_specs=(VMEM,) * 3,
        scratch_shapes=[
            pltpu.VMEM((F, F, CELLS), jnp.bfloat16),
            pltpu.VMEM((GROUPS, 128), jnp.float32),
            pltpu.SMEM((1,), jnp.int32),
            pltpu.SemaphoreType.DMA((3,)),
        ],
        compiler_params=params(50),
        cost_estimate=cost(1000000, 2500000),
        name="prepare",
    )(counts, precond, volume, after)


def live_rows(counts_ref, block):
    cell = lax.broadcasted_iota(jnp.int32, (8, 128), 0) * 128 + lax.broadcasted_iota(jnp.int32, (8, 128), 1)
    return jnp.where(cell + block * 1024 < counts_ref[0], 1.0, 0.0)


def flux_kernel(
    counts_hbm, match_hbm, slide_hbm, psi_hbm, nbr_hbm, target_hbm, jac_hbm, *refs
):
    pieces = refs[:-13]
    (out_ref, psi_s, counts_ref, match_ref, slide_ref, nbr_s, target_s, jac_s, stencil_s, pool_s, ghost_s, part_s, sems) = refs[-13:]
    small = [
        pltpu.make_async_copy(counts_hbm, counts_ref, sems.at[8]),
        pltpu.make_async_copy(match_hbm, match_ref, sems.at[9]),
        pltpu.make_async_copy(slide_hbm, slide_ref, sems.at[10]),
    ]
    nbr_copy = pltpu.make_async_copy(nbr_hbm, nbr_s, sems.at[11])
    psi_copy = pltpu.make_async_copy(psi_hbm, psi_s, sems.at[12])
    target_copy = pltpu.make_async_copy(target_hbm, target_s, sems.at[13])

    def jac_copy(b):
        cells = pl.ds(pl.multiple_of(b * 1024, 1024), 1024)
        return pltpu.make_async_copy(jac_hbm.at[:, :, :, cells], jac_s.at[:, :, :, cells], sems.at[b])

    for copy in small:
        copy.start()
    nbr_copy.start()
    psi_copy.start()
    for b in range(8):
        jac_copy(b).start()
    target_copy.start()
    hops = iter(HOPS)
    for piece in pieces:
        for n in range(piece.shape[0] // 64):
            pool_s[pl.ds(next(hops) * 64, 64), :] = piece[pl.ds(n * 64, 64), :]
    stencil_s[...] = jnp.zeros_like(stencil_s)
    own = lax.axis_index("blk")
    lane = lax.broadcasted_iota(jnp.int32, (8, 128), 1)
    for copy in small:
        copy.wait()
    for q in range(4):
        block = match_ref[q]
        part = block // 4
        hop = (part // 2) ^ (own // 2)
        side = lax.rem(part, 2) ^ lax.rem(own, 2)
        source = pool_s[tile((hop * 8 + side * 4 + lax.rem(block, 4)) * 8), :]
        ghost_s[pl.ds(q * 8, 8), :] = lane_gather(source, (lane + slide_ref[q]) & 127)
    nbr_copy.wait()
    for k in range(K):
        for b in range(8):
            stencil_s[pl.ds(b * 64 + k, 8, stride=8), :] = nbr_s[pl.ds(k * GROUPS + b * 8, 8), :]
    psi_copy.wait()
    for b in range(8):
        live = live_rows(counts_ref, b)
        for f in range(F):
            rows = pl.ds(f * GROUPS + b * 8, 8)
            psi_s[rows, :] = psi_s[rows, :] * live

    def step(b, carry):
        for n in range(UNROLL // 8):
            jac_copy(b * (UNROLL // 8) + n).wait()
        for s in range(UNROLL):
            g = b * UNROLL + s
            at = pl.multiple_of(g * 128, 128)
            index = stencil_s[tile(g * 8), :]
            outside = index >= 128
            pick = index & 127
            total = [None] * F
            for j in range(F):
                inner = jnp.broadcast_to(psi_s[pl.ds(j * GROUPS + g, 1), :], (8, 128))
                outer = jnp.broadcast_to(ghost_s[pl.ds((s % 4) * 8 + j, 1), :], (8, 128))
                value = jnp.where(outside, lane_gather(outer, pick), lane_gather(inner, pick))[:K]
                for i in range(F):
                    term = jac_s[i, j, :, pl.ds(at, 128)].astype(jnp.float32) * value
                    total[i] = term if j == 0 else total[i] + term
            for i in range(F):
                part_s[pl.ds(pl.multiple_of(g * 48 + i * 8, 8), K), :] = total[i]
        return carry

    lax.fori_loop(0, GROUPS // UNROLL, step, 0)
    target_copy.wait()

    def gather_up(b, carry):
        for j in range(F):
            flux = part_s[pl.ds(b * 384 + j * 8, 8, stride=48), :]
            for k in range(1, K):
                flux = flux + part_s[pl.ds(b * 384 + j * 8 + k, 8, stride=48), :]
            rows = tile(j * GROUPS + b * 8)
            out_ref[rows, :] = flux - target_s[rows, :]
        return carry

    lax.fori_loop(0, 8, gather_up, 0, unroll=2)


def flux_part(hint, counts, match, slide, psi, neighbours, target, jac, pieces):
    return pl.pallas_call(
        flux_kernel,
        out_shape=(f32_rows(ROWS), f32_rows(ROWS)),
        in_specs=[ANY] * 7 + [VMEM] * len(pieces),
        out_specs=(VMEM, VMEM),
        scratch_shapes=[
            pltpu.SMEM((1,), jnp.int32),
            pltpu.SMEM((4,), jnp.int32),
            pltpu.SMEM((4,), jnp.int32),
            pltpu.VMEM((ROWS, 128), jnp.int32),
            pltpu.VMEM((ROWS, 128), jnp.float32),
            pltpu.VMEM((F, F, K, CELLS), jnp.bfloat16),
            pltpu.VMEM((GROUPS * 8, 128), jnp.int32),
            pltpu.VMEM((256, 128), jnp.float32),
            pltpu.VMEM((32, 128), jnp.float32),
            pltpu.VMEM((GROUPS * 48, 128), jnp.float32),
            pltpu.SemaphoreType.DMA((14,)),
        ],
        compiler_params=params(50),
        cost_estimate=cost(hint, 7000000),
        name="flux_part",
    )(counts, match, slide, psi, neighbours, target, jac, *pieces)


def couple_kernel(own_ref, other_ref, out_hbm, out_ref, sems):
    def put(n):
        rows = pl.ds(n * 8 * CHUNK, 8 * CHUNK)
        return pltpu.make_async_copy(out_ref.at[rows, :], out_hbm.at[rows, :], sems.at[n])

    f = [float(v) for v in time_kernel()]
    first = lax.rem(lax.axis_index("tm"), 2) == 0
    even = f[0::2]
    odd = [jnp.where(first, f[2 * n + 1], f[2 * n - 1]) for n in range(CHIPS)]
    for t0 in range(0, CHIPS, 8):
        for r in range(CHUNK // 8):
            total = [None] * 8
            for s in range(CHIPS):
                own = own_ref[pl.ds(s * CHUNK + r * 8, 8), :]
                other = other_ref[pl.ds(s * CHUNK + r * 8, 8), :]
                for t in range(8):
                    n = (s - t0 - t) % CHIPS
                    term = even[n] * own + odd[n] * other
                    total[t] = term if s == 0 else total[t] + term
            for t in range(8):
                out_ref[pl.ds((t0 + t) * CHUNK + r * 8, 8), :] = total[t]
        put(t0 // 8).start()
    for n in range(2):
        put(n).wait()


def couple(own, other):
    return pl.pallas_call(
        couple_kernel,
        out_shape=f32_rows(ROWS),
        in_specs=[VMEM, VMEM],
        out_specs=ANY,
        scratch_shapes=[pltpu.VMEM((ROWS, 128), jnp.float32), pltpu.SemaphoreType.DMA((2,))],
        compiler_params=params(),
        cost_estimate=cost(3200000, 600000),
        name="couple",
    )(own, other)


def finish_kernel(base_ref, residual_ref, coupling_ref, live_ref, scale_ref, dense_ref, *rest):
    out_hbm = rest[-3] if len(rest) == 3 else rest[1]
    out_ref, sems = rest[-2:]

    def put(half, f):
        rows = pl.ds(f * GROUPS + half * 32, 32)
        return pltpu.make_async_copy(out_ref.at[rows, :], out_hbm.at[rows, :], sems.at[half * F + f])

    def step(b, carry):
        live = live_ref[tile(b * 8), :]
        scale = scale_ref[tile(b * 8), :]
        whole = []
        for j in range(F):
            rows = tile(j * GROUPS + b * 8)
            whole.append(live * residual_ref[rows, :] + scale * coupling_ref[rows, :])
        for i in range(F):
            rows = tile(i * GROUPS + b * 8)
            value = base_ref[rows, :]
            for j in range(F):
                value = value - dense_ref[tile((i * F + j) * STRIDE + b * 8), :] * whole[j]
            out_ref[rows, :] = value
        return carry

    for half in range(2):
        lax.fori_loop(half * 4, half * 4 + 4, step, 0, unroll=2)
        for f in range(F):
            put(half, f).start()
    if len(rest) > 3:
        donor_kernel(out_ref, rest[0], rest[2])
    for half in range(2):
        for f in range(F):
            put(half, f).wait()


def finish(base, residual, coupling, live, scale, dense, donor=None):
    operands = [base, residual, coupling, live, scale, dense] + ([] if donor is None else [donor])
    shapes = [f32_rows(ROWS)] + ([] if donor is None else [f32_rows(32)])
    return pl.pallas_call(
        finish_kernel,
        out_shape=shapes,
        in_specs=[VMEM] * len(operands),
        out_specs=[ANY, VMEM][: len(shapes)],
        scratch_shapes=[pltpu.VMEM((ROWS, 128), jnp.float32), pltpu.SemaphoreType.DMA((2 * F,))],
        compiler_params=params(),
        cost_estimate=cost(600000, 2000000),
        name="finish",
    )(*operands)


def local(
    psi_start, objective, jacobian, precond, volume, counts, neighbours, donor, match_block, slide
):
    by_core = [[2 * chip + core for chip in range(CHIPS)] for core in range(2)]
    swap_core = [(i, i ^ 1) for i in range(NT)]

    def across(x):
        moved = lax.all_to_all(x.reshape(CHIPS, CHUNK, 128), "tm", 0, 0, axis_index_groups=by_core)
        return moved.reshape(ROWS, 128)
    def blk_swap(x, bits):
        return lax.ppermute(x, "blk", [(i, i ^ bits) for i in range(8)])

    psi = psi_start.reshape(ROWS, 128)
    target = objective.reshape(ROWS, 128)
    faces = donor.reshape(4, 128)
    nearby = neighbours.reshape(ROWS, 128)
    match, slides = match_block.reshape(4), slide.reshape(4)
    sent = pack_donors(psi, faces)
    for sweep in range(SWEEPS):
        both = merge(MERGEHINTS[sweep], [sent, blk_swap(sent, 1)], [counts] if sweep == 0 else [])
        pieces = [both] + [blk_swap(both, 2 * hop) for hop in HOPS[1:]]
        if sweep == 0:
            psi, sent = lax.optimization_barrier((psi, sent))
        states = across(psi)
        states, pieces[0] = lax.optimization_barrier((states, pieces[0]))
        coupling = across(couple(states, lax.ppermute(states, "tm", swap_core)))
        residual, base = flux_part(FLUXHINTS[sweep], counts, match, slides, psi, nearby, target, jacobian[0, 0], pieces)
        if sweep == 0:
            dense, live, scale = prepare(counts, precond[0, 0], volume.reshape(GROUPS, 128), residual)
        more = [faces] if sweep + 1 < SWEEPS else []
        psi, *rest = finish(base, residual, coupling, live, scale, dense, *more)
        if rest:
            sent = rest[0]
    return psi.reshape(1, 1, F, CELLS)


def solution(mesh):
    in_specs = (
        P("tm", "blk", None, None),
        P("tm", "blk", None, None),
        P("tm", "blk", None, None, None, None),
        P("tm", "blk", None, None, None),
        P("blk", None),
        P("blk"),
        P("blk", None, None),
        P("blk", None),
        P("tm", "blk", None),
        P("tm", "blk", None),
    )
    out_specs = P("tm", "blk", None, None)
    return jax.shard_map(local, mesh=mesh, in_specs=in_specs, out_specs=out_specs, check_vma=False)
```
